32 devices in a mesh: groups: 2 (over y), expert: 16 (over z, x, core).
Axes of the slice: x: 2, y: 2, z: 4, core: 2. Of those that a mesh axis runs over, the one named last changes fastest.
Arguments:
- tokens: bfloat16 [1024, 3584], P(('groups', 'expert')), parts along dimension 0, may hold values from -6 to 6
- norm_gain: float32 [3584], replicated, may hold values from 0.5 to 2
- pred_ids: int32 [1024, 8], P(('groups', 'expert')), parts along dimension 0, may hold values from 0 to 15, all different within a row; in each aligned block of 32 rows (0 to 31, 32 to 63, ...) at most 17 rows name the same one
- pred_weights: float32 [1024, 8], P(('groups', 'expert')), parts along dimension 0, may hold values from 0.1 to 1
- fix_pairs: int32 [2048], P(('groups', 'expert')), parts along dimension 0, may hold values from 0 to 4095, as said below
- fix_ids: int32 [2048, 1], P(('groups', 'expert')), parts along dimension 0, may hold values from 0 to 15; in each aligned block of 64 rows (0 to 63, 64 to 127, ...) at most 5 rows name the same one
- fix_weights: float32 [2048], P(('groups', 'expert')), parts along dimension 0, may hold values from 0.1 to 1
- w_expert: bfloat16 [16, 3584, 1024], P('expert'), may hold values from -0.09375 to 0.09375
Outputs:
- mixed: float32 [1024, 1024], P(('groups', 'expert')), parts along dimension 0
The draws below stay inside these ranges and needn't reach their ends.
There are 2 independent parts, one for each index of `groups`. The reference program is written for one: setup_inputs(seed, part) draws one part's arguments, and reference() takes and returns one part's arrays. A program takes and returns all parts, laid end to end along the dimension named above; an argument that names none is the same for every part. Nothing has to cross between parts.
Inputs may be any that keep to these rules, and one draw needn't show every extreme that they name: `pred_ids`: each token names 8 different experts; within the 32 tokens of one device no expert is named by more than 17 of them. `fix_pairs`: the 64 entries of the i-th aligned block are distinct pairs of the tokens of the i-th aligned block of 32 tokens. `fix_ids`: within each aligned block of 64 entries no expert is named more than 5 times.
All inputs are finite; a program needn't handle non-finite values.
Results may differ from the reference program's by a relative error of at most 0.0034.
Values may be sent and summed in bfloat16 or wider, within the bound.
A program may use at most 64 MiB of HBM per device.

```python
import math
import jax
import jax.numpy as jnp
import numpy as np
from jax import lax

D = 3584
FFW = 1024
TOP = 8
TOK_DEV = 32
EXPERTS = 16
TOKENS = 512
FIX_DEV = 64
FIXES = 1024
CAP = 17
FCAP = 5
N_EXPERT = 16


def draw_fix_pairs(key, part):
    key = jax.random.fold_in(key, 11)
    block_count = FIXES // FIX_DEV
    block_keys = jax.random.split(key, block_count)
    chosen = jax.vmap(lambda one_key: jax.random.permutation(one_key, TOK_DEV * TOP)[:FIX_DEV])(block_keys)
    offsets = jnp.arange(block_count, dtype=jnp.int32)[:, None] * (TOK_DEV * TOP)
    return (chosen.astype(jnp.int32) + offsets).reshape(-1).astype(jnp.int32)


def levels(own_key, extent, pieces, low, high):
    gain, own = 1.0, jax.random.fold_in(own_key, 6)
    for dim, blocks in pieces:
        steps = jnp.exp(jax.random.uniform(jax.random.fold_in(own, dim), (blocks,), jnp.float32, low / len(pieces), high / len(pieces)))
        gain = gain * jnp.repeat(steps, extent[dim] // blocks).reshape([-1 if axis == dim else 1 for axis in range(len(extent))])
    return gain


def assign_block(own_key, own, number, rows, number_of, top, limit, slope):
    ranking = jax.random.permutation(own_key, number_of)
    packed, ordinary = shares(number_of, rows * top, limit, slope, True), shares(number_of, rows * top, limit, slope, False)
    places = jnp.arange(number_of)

    def named(tallies, offset_by):
        used = int((tallies > 0).sum())
        fixed = max(1, used // 4)
        shifted = fixed + (places - fixed + offset_by * (used - fixed)) % max(1, number_of - fixed)
        return jnp.zeros((number_of,), jnp.int32).at[ranking[jnp.where(places < fixed, places, shifted)]].set(jnp.asarray(tallies, jnp.int32))

    tallies = jnp.where(number % 4 == 0, named(packed, number // 4), named(ordinary, number - number // 4 - 1))
    mixed = jax.random.permutation(jax.random.fold_in(own, 3), number_of)
    source_of, receiver = mixed[0:number_of // 2 * 2:2], mixed[1:number_of // 2 * 2:2]
    slack = jnp.minimum(tallies[source_of] - 1, limit - tallies[receiver]) // 2
    slack = jnp.where((source_of == ranking[0]) | (receiver == ranking[0]) | (tallies[receiver] == 0), 0, jnp.maximum(slack, 0))
    shifted = jax.random.randint(jax.random.fold_in(own, 4), (number_of // 2,), 0, 1 << 20) % (slack + 1)
    tallies = tallies.at[source_of].add(-shifted).at[receiver].add(shifted)
    labels = jnp.searchsorted(jnp.cumsum(tallies), jnp.arange(rows * top), side="right").astype(jnp.int32)
    listing = labels.reshape(top, rows).T
    listing = listing[jax.random.permutation(jax.random.fold_in(own, 1), rows)]
    offset_by = jax.random.randint(jax.random.fold_in(own, 2), (rows, 1), 0, top)
    return jnp.take_along_axis(listing, (jnp.arange(top)[None, :] + offset_by) % top, axis=1)


def shares(number_of, total, most, skew, full):
    portions = [(1 << 20) // math.isqrt(grade ** skew) + 1 for grade in range(1, number_of + 1)]
    largest = most if full else min(most, max(-(-total // number_of), total * portions[0] // sum(portions)))
    least = 1 if total - largest >= number_of - 1 else 0
    given, rest = [largest] + [least] * (number_of - 1), total - largest - least * (number_of - 1)
    while rest > 0:
        free = [i for i in range(1, number_of) if given[i] < largest] or [i for i in range(1, number_of) if given[i] < most]
        pool, budget = sum([portions[i] for i in free]), rest
        for i in free:
            more = min(most - given[i], max(1, budget * portions[i] // pool), rest)
            given[i] = given[i] + more
            rest = rest - more
    return np.array(given)


def centred(rng, extent, scale, reach, cuts=(), kind=jnp.bfloat16):
    factor_of = levels(rng, extent, cuts, -0.22, 0.18) if cuts else 1.0
    result = jax.random.normal(rng, extent, jnp.float32) * scale * factor_of
    return jnp.minimum(jnp.maximum(result, -reach), reach).astype(kind)


def setup_inputs(seed: int = 0, part: int = 0) -> dict:
    key_list = jax.random.split(jax.random.key(seed), 9)
    own_keys = jax.random.split(jax.random.fold_in(key_list[8], part), 9)
    tokens = centred(own_keys[0], (TOKENS, D), 1.0, 6.0, ((0, 16),))
    norm_gain = jnp.clip(jnp.exp(jax.random.uniform(key_list[1], (D,), jnp.float32, math.log(0.5), math.log(2.0))), 0.5, 2.0)
    pred_ids_keys = jax.random.split(jax.random.fold_in(own_keys[2], 1), TOKENS // TOK_DEV)
    pred_ids_turns = jax.random.permutation(jax.random.fold_in(own_keys[2], 3), TOKENS // TOK_DEV)
    pred_ids = jax.vmap(lambda own, number: assign_block(jax.random.fold_in(own_keys[2], 2), own, number, TOK_DEV, EXPERTS, TOP, CAP, 2))(pred_ids_keys, pred_ids_turns).reshape((TOKENS, TOP))
    pred_weights = jnp.clip(jnp.exp(math.log(1.0) - 2.3025851 * jax.random.uniform(own_keys[3], (TOKENS, TOP), jnp.float32) ** levels(own_keys[3], (TOKENS, TOP), ((0, 16),), -0.2, 0.2)), 0.1, 1.0)
    fix_pairs = draw_fix_pairs(jax.random.fold_in(jax.random.fold_in(key_list[8], part), 71), part)
    fix_ids_keys = jax.random.split(jax.random.fold_in(own_keys[5], 1), FIXES // FIX_DEV)
    fix_ids_turns = jax.random.permutation(jax.random.fold_in(own_keys[5], 3), FIXES // FIX_DEV)
    fix_ids = jax.vmap(lambda own, number: assign_block(jax.random.fold_in(own_keys[5], 2), own, number, FIX_DEV, EXPERTS, 1, FCAP, 2))(fix_ids_keys, fix_ids_turns).reshape((FIXES, 1))
    fix_weights = jnp.clip(jnp.exp(math.log(1.0) - 2.3025851 * jax.random.uniform(own_keys[6], (FIXES,), jnp.float32) ** levels(own_keys[6], (FIXES,), ((0, 16),), -0.2, 0.2)), 0.1, 1.0)
    w_expert = centred(key_list[7], (EXPERTS, D, FFW), D ** -0.5, 0.09375, ((0, 16),))
    return dict(tokens=tokens, norm_gain=norm_gain, pred_ids=pred_ids, pred_weights=pred_weights, fix_pairs=fix_pairs, fix_ids=fix_ids, fix_weights=fix_weights, w_expert=w_expert)


def reference(tokens, norm_gain, pred_ids, pred_weights, fix_pairs, fix_ids, fix_weights, w_expert):
    widened = tokens.astype(jnp.float32)
    normed = (widened * lax.rsqrt(lax.optimization_barrier(jnp.mean(widened * widened, axis=-1, keepdims=True)) + 1e-06) * norm_gain).astype(jnp.bfloat16)
    route_ids = pred_ids.reshape(-1).at[fix_pairs].set(fix_ids[:, 0])
    route_weights = pred_weights.reshape(-1).at[fix_pairs].set(fix_weights)
    pair_total = route_ids.shape[0]
    sort_order = jnp.argsort(route_ids, stable=True).astype(jnp.int32)
    expert_counts = jax.ops.segment_sum(jnp.ones_like(route_ids), route_ids, num_segments=EXPERTS).astype(jnp.int32)
    expert_starts = (jnp.cumsum(expert_counts) - expert_counts).astype(jnp.int32)
    row_bound = N_EXPERT * (CAP + FCAP)
    row_range = jnp.arange(row_bound, dtype=jnp.int32)

    def per_expert(total, expert):
        position = expert_starts[expert] + row_range
        is_valid = row_range < expert_counts[expert]
        picked = sort_order[jnp.minimum(position, pair_total - 1)]
        token_of = (picked // TOP).astype(jnp.int32)
        hidden = jnp.dot(normed[token_of], w_expert[expert], preferred_element_type=jnp.float32)
        expert_out = lax.optimization_barrier(jax.nn.silu(hidden).astype(jnp.bfloat16)).astype(jnp.float32)
        pair_scale = jnp.where(is_valid, route_weights[picked], jnp.zeros_like(route_weights[picked]))
        return (total.at[token_of].add(pair_scale[:, None] * expert_out), None)
    mixed, _ = lax.scan(per_expert, jnp.zeros((TOKENS, FFW), jnp.float32), jnp.arange(EXPERTS, dtype=jnp.int32))
    return mixed
```

```python
import functools

import jax
import jax.numpy as jnp
from jax import lax
from jax.experimental import pallas as pl
from jax.experimental.pallas import tpu as pltpu
from jax.sharding import PartitionSpec as P

MESH = pl.DeviceIdType.MESH
QUAD = 4
RING = 4
RIGHT, LEFT, ACROSS, SIB, SIB_X, RS1, RS2, RS3 = range(8)


def route_columns(peers, width, pid_ref, pw_ref, fp_ref, fid_ref, fw_ref):
    tok_rows, top_k = pid_ref.shape
    fixes = fp_ref.shape[1]
    pairs = lax.rem(fp_ref[...], tok_rows * top_k)
    pair_tok = lax.div(pairs, top_k)
    pair_slot = lax.rem(pairs, top_k)
    row = lax.broadcasted_iota(jnp.int32, (tok_rows, fixes), 0)
    owned = row == pair_tok
    lane = lax.broadcasted_iota(jnp.int32, (tok_rows, width), 1)
    expert = lax.rem(lane, peers)
    piece = lax.div(lane, peers)
    fix_lane = lax.rem(lax.broadcasted_iota(jnp.int32, (fixes, width), 1), peers)
    hits = jnp.where(fid_ref[...] == fix_lane, 1.0, 0.0).astype(jnp.float32)
    share = jnp.where(owned, jnp.broadcast_to(fw_ref[...], (tok_rows, fixes)), 0.0)
    total = jnp.dot(share, hits, precision=lax.Precision.HIGHEST, preferred_element_type=jnp.float32)
    pids = pid_ref[...]
    weights = pw_ref[...]
    for k in range(top_k):
        gone = jnp.max(jnp.where(owned & (pair_slot == k), 1.0, 0.0), axis=1, keepdims=True)
        keep = weights[:, k : k + 1] * (1.0 - gone)
        total = total + jnp.where(pids[:, k : k + 1] == expert, keep, 0.0)
    high = total.astype(jnp.bfloat16).astype(jnp.float32)
    rest = total - high
    mid = rest.astype(jnp.bfloat16).astype(jnp.float32)
    low = rest - mid
    picked = jnp.where(piece == 0, high, jnp.where(piece == 1, mid, jnp.where(piece == 2, low, 0.0)))
    return picked.astype(jnp.bfloat16)


def kernel(
    peers,
    tok_ref,
    gain_ref,
    pid_ref,
    pw_ref,
    fp_ref,
    fid_ref,
    fw_ref,
    w_hbm,
    out_ref,
    xbuf,
    wbuf,
    ybuf,
    acc,
    own,
    s1,
    r1,
    s2,
    r2,
    s3,
    r3,
    w_sem,
    snd,
    rcv,
    rs_rcv,
):
    line = peers // QUAD
    tok_rows, feats = tok_ref.shape
    hidden = wbuf.shape[1]
    width = xbuf.shape[2] - feats
    group = lax.axis_index("groups")
    me = lax.axis_index("expert")
    o = me // QUAD
    x = (me % QUAD) // 2
    c = me % 2

    def dev(o_, x_, c_):
        return (group, o_ * QUAD + x_ * 2 + c_)

    w_copy = pltpu.make_async_copy(w_hbm.at[0], wbuf, w_sem)
    w_copy.start()

    barrier = pltpu.get_barrier_semaphore()
    pl.semaphore_signal(barrier, inc=1, device_id=dev(o, 1 - x, c), device_id_type=MESH)
    pl.semaphore_signal(barrier, inc=1, device_id=dev(o, x, 1 - c), device_id_type=MESH)
    for d in range(1, line):
        pl.semaphore_signal(
            barrier, inc=1, device_id=dev((o + d) % line, x, c), device_id_type=MESH
        )

    wide = tok_ref[...].astype(jnp.float32)
    scale = lax.rsqrt(jnp.mean(wide * wide, axis=-1, keepdims=True) + 1e-06)
    xbuf[me, :, 0:feats] = (wide * scale * gain_ref[...]).astype(jnp.bfloat16)
    xbuf[me, :, feats : feats + width] = route_columns(
        peers, width, pid_ref, pw_ref, fp_ref, fid_ref, fw_ref
    )
    pl.semaphore_wait(barrier, line + 1)

    def quad_at(p):
        m = jnp.minimum(o, line - 1 - o)
        near = jnp.where(p % 2 == 1, o - (p + 1) // 2, o + p // 2)
        far = jnp.where(o < line - 1 - o, p, line - 1 - p)
        return jnp.where(p <= 2 * m, near, far)

    def send(src, dst, kind, p, recv, device):
        return pltpu.make_async_remote_copy(
            src_ref=src,
            dst_ref=dst,
            send_sem=snd.at[kind, p],
            recv_sem=recv,
            device_id=device,
            device_id_type=MESH,
        )

    def block(e, kind, p, device):
        return send(xbuf.at[e], xbuf.at[e], kind, p, rcv.at[e], device)

    def rail(p):
        return quad_at(p) * QUAD + x * 2 + c

    def crossed(p):
        return quad_at(p) * QUAD + (1 - x) * 2 + c

    def goes_right(p):
        return (quad_at(p) <= o) & (o < line - 1)

    def goes_left(p):
        return (quad_at(p) >= o) & (o > 0)

    right = dev(jnp.minimum(o + 1, line - 1), x, c)
    left = dev(jnp.maximum(o - 1, 0), x, c)
    across = dev(o, 1 - x, c)
    sib = dev(o, x, 1 - c)

    def rs1(p):
        return send(s1.at[p], r1.at[p], RS1, p, rs_rcv.at[0, p], sib)

    def rs2(p):
        return send(s2.at[p], r2.at[p], RS2, p, rs_rcv.at[1, p], across)

    def rs3(p):
        return send(s3.at[p], r3.at[o], RS3, p, rs_rcv.at[2, o], dev(quad_at(p), x, c))

    def step_a(p):
        e = rail(p)

        @pl.when(p > 0)
        def _():
            block(e, SIB, p, sib).wait_recv()

        @pl.when(goes_right(p))
        def _():
            block(e, RIGHT, p, right).start()

        @pl.when(goes_left(p))
        def _():
            block(e, LEFT, p, left).start()

        block(e, ACROSS, p, across).start()
        block(e, SIB, p, sib).start()

    def step_b(p):
        e = crossed(p)
        block(e, SIB_X, p, sib).wait_recv()
        block(e, SIB_X, p, sib).start()

    def step_c(p):
        q = quad_at(p)
        block(q * QUAD + x * 2 + 1 - c, SIB, p, sib).wait_recv()
        block(q * QUAD + (1 - x) * 2 + 1 - c, SIB_X, p, sib).wait_recv()

        @pl.when(p == 0)
        def _():
            w_copy.wait()

        rows = QUAD * tok_rows
        slot = p % RING
        extra = xbuf[pl.ds(q * QUAD, QUAD), :, feats : feats + width].reshape(rows, width)
        lane = lax.broadcasted_iota(jnp.int32, (rows, width), 1)
        mine = (lax.rem(lane, peers) == me) & (lane < 3 * peers)
        share = jnp.sum(jnp.where(mine, extra.astype(jnp.float32), 0.0), axis=1, keepdims=True)
        tile = 256

        def column(j, carry):
            cols = pl.ds(pl.multiple_of(j * tile, tile), tile)
            lhs = xbuf[pl.ds(q * QUAD, QUAD), :, 0:feats].reshape(rows, feats)
            h = jnp.dot(lhs, wbuf[:, cols], preferred_element_type=jnp.float32)
            y = (h / (1.0 + jnp.exp(-h))).astype(jnp.bfloat16).astype(jnp.float32) * share
            ybuf[slot, :, :, cols] = y.reshape(QUAD, tok_rows, tile)
            return carry

        lax.fori_loop(0, hidden // tile, column, 0)
        for k in range(2):
            s1[p, k] = ybuf[slot, k * 2 + 1 - c].astype(jnp.bfloat16)
        rs1(p).start()

    def step_d(p):
        slot = p % RING
        rs1(p).wait_recv()
        s2[p] = (ybuf[slot, (1 - x) * 2 + c] + r1[p, 1 - x].astype(jnp.float32)).astype(jnp.bfloat16)
        rs2(p).start()
        acc[slot] = ybuf[slot, x * 2 + c] + r1[p, x].astype(jnp.float32)

    def step_e(p):
        slot = p % RING
        rs2(p).wait_recv()

        @pl.when(quad_at(p) == o)
        def _():
            own[...] = acc[slot] + r2[p].astype(jnp.float32)

        @pl.when(quad_at(p) != o)
        def _():
            s3[p] = (acc[slot] + r2[p].astype(jnp.float32)).astype(jnp.bfloat16)
            rs3(p).start()

    def step(i, carry):
        @pl.when(i < line)
        def _():
            step_a(i)

        @pl.when((i >= 1) & (i < line + 1))
        def _():
            step_b(i - 1)
            step_c(i - 1)

        @pl.when((i >= 2) & (i < line + 2))
        def _():
            step_d(i - 2)

        @pl.when(i >= 3)
        def _():
            step_e(i - 3)

        return carry

    lax.fori_loop(0, line + 3, step, 0)

    for d in range(1, line):
        k = (o + d) % line
        send(s3.at[0], r3.at[k], RS3, 0, rs_rcv.at[2, k], sib).wait_recv()
        own[...] += r3[k].astype(jnp.float32)
    out_ref[...] = own[...]

    def drain(p, carry):
        @pl.when(goes_right(p))
        def _():
            block(rail(p), RIGHT, p, right).wait_send()

        @pl.when(goes_left(p))
        def _():
            block(rail(p), LEFT, p, left).wait_send()

        block(rail(p), ACROSS, p, across).wait_send()
        block(rail(p), SIB, p, sib).wait_send()
        block(crossed(p), SIB_X, p, sib).wait_send()
        rs1(p).wait_send()
        rs2(p).wait_send()

        @pl.when(quad_at(p) != o)
        def _():
            rs3(p).wait_send()

        return carry

    lax.fori_loop(0, line, drain, 0)


def body(tokens, norm_gain, pred_ids, pred_weights, fix_pairs, fix_ids, fix_weights, w_expert):
    peers = lax.axis_size("expert")
    line = peers // QUAD
    tok_rows, feats = tokens.shape
    hidden = w_expert.shape[2]
    width = -(-3 * peers // 128) * 128
    vmem = pl.BlockSpec(memory_space=pltpu.VMEM)
    bf16 = jnp.bfloat16
    return pl.pallas_call(
        functools.partial(kernel, peers),
        out_shape=jax.ShapeDtypeStruct((tok_rows, hidden), jnp.float32),
        in_specs=[vmem] * 7 + [pl.BlockSpec(memory_space=pl.ANY)],
        out_specs=vmem,
        scratch_shapes=[
            pltpu.VMEM((peers, tok_rows, feats + width), bf16),
            pltpu.VMEM((feats, hidden), bf16),
            pltpu.VMEM((RING, QUAD, tok_rows, hidden), jnp.float32),
            pltpu.VMEM((RING, tok_rows, hidden), jnp.float32),
            pltpu.VMEM((tok_rows, hidden), jnp.float32),
            pltpu.VMEM((line, 2, tok_rows, hidden), bf16),
            pltpu.VMEM((line, 2, tok_rows, hidden), bf16),
            pltpu.VMEM((line, tok_rows, hidden), bf16),
            pltpu.VMEM((line, tok_rows, hidden), bf16),
            pltpu.VMEM((line, tok_rows, hidden), bf16),
            pltpu.VMEM((line, tok_rows, hidden), bf16),
            pltpu.SemaphoreType.DMA,
            pltpu.SemaphoreType.DMA((8, line)),
            pltpu.SemaphoreType.DMA((peers,)),
            pltpu.SemaphoreType.DMA((3, line)),
        ],
        compiler_params=pltpu.CompilerParams(
            collective_id=0, has_side_effects=True, vmem_limit_bytes=62 * 2**20
        ),
    )(
        tokens,
        norm_gain.reshape(1, feats),
        pred_ids,
        pred_weights,
        fix_pairs.reshape(1, -1),
        fix_ids,
        fix_weights.reshape(1, -1),
        w_expert,
    )


def solution(mesh):
    in_specs = (
        P(("groups", "expert"), None),
        P(),
        P(("groups", "expert"), None),
        P(("groups", "expert"), None),
        P(("groups", "expert")),
        P(("groups", "expert"), None),
        P(("groups", "expert")),
        P("expert", None, None),
    )
    out_specs = P(("groups", "expert"), None)
    return jax.shard_map(body, mesh=mesh, in_specs=in_specs, out_specs=out_specs, check_vma=False)
```

```python
import functools

import jax
import jax.numpy as jnp
from jax import lax
from jax.experimental import pallas as pl
from jax.experimental.pallas import tpu as pltpu
from jax.sharding import PartitionSpec as P

MESH = pl.DeviceIdType.MESH
QUAD = 4
RING = 4
RIGHT, LEFT, ACROSS, SIB, SIB_X, RS1, RS2, RS3 = range(8)
PIECES = 2


def route_columns(peers, width, pid_ref, pw_ref, fp_ref, fid_ref, fw_ref):
    top_k, tok_rows = pid_ref.shape
    fixes = fp_ref.shape[1]
    last = (((1,), (1,)), ((), ()))
    pairs = lax.rem(fp_ref[...], tok_rows * top_k)
    owned = lax.broadcasted_iota(jnp.int32, (tok_rows, fixes), 0) == lax.div(pairs, top_k)
    slots = lax.broadcasted_iota(jnp.int32, (top_k, fixes), 0) == lax.rem(pairs, top_k)
    gone = lax.dot_general(
        jnp.where(slots, 1.0, 0.0),
        jnp.where(owned, 1.0, 0.0),
        last,
        preferred_element_type=jnp.float32,
    )
    keep = jnp.where(gone > 0.5, 0.0, pw_ref[...])
    pids = pid_ref[...]
    row = lax.broadcasted_iota(jnp.int32, (width, tok_rows), 0)
    expert = lax.rem(row, peers)
    piece = lax.div(row, peers)
    fix_row = lax.rem(lax.broadcasted_iota(jnp.int32, (width, fixes), 0), peers)
    hits = jnp.where(fid_ref[...] == fix_row, 1.0, 0.0)
    share = jnp.where(owned, jnp.broadcast_to(fw_ref[...], (tok_rows, fixes)), 0.0)
    total = lax.dot_general(
        hits,
        share,
        last,
        precision=lax.Precision.HIGHEST,
        preferred_element_type=jnp.float32,
    )
    for k in range(top_k):
        total = total + jnp.where(pids[k : k + 1, :] == expert, keep[k : k + 1, :], 0.0)
    high = total.astype(jnp.bfloat16).astype(jnp.float32)
    rest = total - high
    mid = rest.astype(jnp.bfloat16).astype(jnp.float32)
    low = rest - mid
    picked = jnp.where(piece == 0, high, jnp.where(piece == 1, mid, jnp.where(piece == 2, low, 0.0)))
    side = (tok_rows, tok_rows)
    same = lax.broadcasted_iota(jnp.int32, side, 0) == lax.broadcasted_iota(jnp.int32, side, 1)
    turned = lax.dot_general(
        jnp.where(same, 1.0, 0.0).astype(jnp.bfloat16),
        picked.astype(jnp.bfloat16),
        last,
        preferred_element_type=jnp.float32,
    )
    return turned.astype(jnp.bfloat16)


def kernel(
    peers,
    tok_ref,
    gain_ref,
    pid_ref,
    pw_ref,
    fp_ref,
    fid_ref,
    fw_ref,
    w_hbm,
    out_ref,
    xa,
    xb,
    wbuf,
    hbuf,
    ybuf,
    acc,
    own,
    s1,
    r1,
    s2,
    r2,
    s3,
    r3,
    w_sem,
    snd,
    rcv,
    rs_rcv,
):
    line = peers // QUAD
    tok_rows, feats = tok_ref.shape
    hidden = wbuf.shape[1]
    half = feats // PIECES
    width = xb.shape[2] - half
    pieces = (xa, xb)
    group = lax.axis_index("groups")
    me = lax.axis_index("expert")
    o = me // QUAD
    x = (me % QUAD) // 2
    c = me % 2

    def dev(o_, x_, c_):
        return (group, o_ * QUAD + x_ * 2 + c_)

    w_copy = pltpu.make_async_copy(w_hbm.at[0], wbuf, w_sem)
    w_copy.start()

    barrier = pltpu.get_barrier_semaphore()
    pl.semaphore_signal(barrier, inc=1, device_id=dev(o, 1 - x, c), device_id_type=MESH)
    pl.semaphore_signal(barrier, inc=1, device_id=dev(o, x, 1 - c), device_id_type=MESH)
    for d in range(1, line):
        pl.semaphore_signal(
            barrier, inc=1, device_id=dev((o + d) % line, x, c), device_id_type=MESH
        )

    wide = tok_ref[...].astype(jnp.float32)
    scale = lax.rsqrt(jnp.mean(wide * wide, axis=-1, keepdims=True) + 1e-06)
    gain = gain_ref[...].reshape(1, feats)
    xa[me] = (wide[:, :half] * scale * gain[:, :half]).astype(jnp.bfloat16)
    pl.semaphore_wait(barrier, line + 1)

    def quad_at(p):
        m = jnp.minimum(o, line - 1 - o)
        near = jnp.where(p % 2 == 1, o - (p + 1) // 2, o + p // 2)
        far = jnp.where(o < line - 1 - o, p, line - 1 - p)
        return jnp.where(p <= 2 * m, near, far)

    def send(src, dst, kind, recv, device):
        return pltpu.make_async_remote_copy(
            src_ref=src,
            dst_ref=dst,
            send_sem=kind,
            recv_sem=recv,
            device_id=device,
            device_id_type=MESH,
        )

    def block(e, kind, p, h, device):
        piece = pieces[h].at[e]
        return send(piece, piece, snd.at[h, kind, p], rcv.at[h, e], device)

    def rail(p):
        return quad_at(p) * QUAD + x * 2 + c

    def crossed(p):
        return quad_at(p) * QUAD + (1 - x) * 2 + c

    def goes_right(p):
        return (quad_at(p) <= o) & (o < line - 1)

    def goes_left(p):
        return (quad_at(p) >= o) & (o > 0)

    right = dev(jnp.minimum(o + 1, line - 1), x, c)
    left = dev(jnp.maximum(o - 1, 0), x, c)
    across = dev(o, 1 - x, c)
    sib = dev(o, x, 1 - c)

    def rs1(p):
        return send(s1.at[p], r1.at[p], snd.at[0, RS1, p], rs_rcv.at[0, p], sib)

    def rs2(p):
        return send(s2.at[p], r2.at[p], snd.at[0, RS2, p], rs_rcv.at[1, p], across)

    def rs3(p):
        return send(
            s3.at[p], r3.at[o], snd.at[0, RS3, p], rs_rcv.at[2, o], dev(quad_at(p), x, c)
        )

    def forward(p, h):
        e = rail(p)
        block(e, ACROSS, p, h, across).start()

        @pl.when(goes_right(p))
        def _():
            block(e, RIGHT, p, h, right).start()

        @pl.when(goes_left(p))
        def _():
            block(e, LEFT, p, h, left).start()

        block(e, SIB, p, h, sib).start()

    def step_a(p, h):
        block(rail(p), SIB, p, h, sib).wait_recv()
        forward(p, h)

    def step_b(p, h):
        e = crossed(p)
        block(e, SIB_X, p, h, sib).wait_recv()
        block(e, SIB_X, p, h, sib).start()

    rows = QUAD * tok_rows
    tile = 256

    def step_c(p, h):
        q = quad_at(p)
        block(q * QUAD + x * 2 + 1 - c, SIB, p, h, sib).wait_recv()
        block(q * QUAD + (1 - x) * 2 + 1 - c, SIB_X, p, h, sib).wait_recv()
        quad = pl.ds(q * QUAD, QUAD)
        slot = p % RING
        if h == 0:

            @pl.when(p == 0)
            def _():
                w_copy.wait()

        else:
            extra = xb[quad, :, half : half + width].reshape(rows, width)
            lane = lax.broadcasted_iota(jnp.int32, (rows, width), 1)
            mine = (lax.rem(lane, peers) == me) & (lane < 3 * peers)
            share = jnp.sum(jnp.where(mine, extra.astype(jnp.float32), 0.0), axis=1, keepdims=True)

        def column(j, carry):
            cols = pl.ds(pl.multiple_of(j * tile, tile), tile)
            lhs = pieces[h][quad, :, 0:half].reshape(rows, half)
            part = jnp.dot(
                lhs, wbuf[h * half : (h + 1) * half, cols], preferred_element_type=jnp.float32
            )
            if h == 0:
                hbuf[:, cols] = part
            else:
                v = hbuf[:, cols] + part
                y = (v / (1.0 + jnp.exp(-v))).astype(jnp.bfloat16).astype(jnp.float32) * share
                ybuf[slot, :, :, cols] = y.reshape(QUAD, tok_rows, tile)
            return carry

        lax.fori_loop(0, hidden // tile, column, 0)
        if h == 1:
            for k in range(2):
                s1[p, k] = ybuf[slot, k * 2 + 1 - c].astype(jnp.bfloat16)
            rs1(p).start()

    def step_d(p):
        slot = p % RING
        rs1(p).wait_recv()
        s2[p] = (ybuf[slot, (1 - x) * 2 + c] + r1[p, 1 - x].astype(jnp.float32)).astype(jnp.bfloat16)
        rs2(p).start()
        acc[slot] = ybuf[slot, x * 2 + c] + r1[p, x].astype(jnp.float32)

    def step_e(p):
        slot = p % RING
        rs2(p).wait_recv()

        @pl.when(quad_at(p) == o)
        def _():
            own[...] = acc[slot] + r2[p].astype(jnp.float32)

        @pl.when(quad_at(p) != o)
        def _():
            s3[p] = (acc[slot] + r2[p].astype(jnp.float32)).astype(jnp.bfloat16)
            rs3(p).start()

    def step(i, carry):
        for h in range(PIECES):

            @pl.when(i < line)
            def _():
                step_a(i, h)

            @pl.when(i < line + 1)
            def _():
                step_b(i - 1, h)

            if h == 0:

                @pl.when((i >= 2) & (i < line + 2))
                def _():
                    step_c(i - 2, 1)

            else:

                @pl.when(i < line + 1)
                def _():
                    step_c(i - 1, 0)

        @pl.when((i >= 2) & (i < line + 2))
        def _():
            step_d(i - 2)

        @pl.when(i >= 3)
        def _():
            step_e(i - 3)

        return carry

    forward(0, 0)
    xb[me, :, 0:half] = (wide[:, half:] * scale * gain[:, half:]).astype(jnp.bfloat16)
    xb[me, :, half : half + width] = route_columns(
        peers, width, pid_ref, pw_ref, fp_ref, fid_ref, fw_ref
    )
    forward(0, 1)
    lax.fori_loop(1, line + 3, step, 0)

    for d in range(1, line):
        k = (o + d) % line
        send(s3.at[0], r3.at[k], snd.at[0, RS3, 0], rs_rcv.at[2, k], sib).wait_recv()
        own[...] += r3[k].astype(jnp.float32)
    out_ref[...] = own[...]

    def drain(p, carry):
        for h in range(PIECES):

            @pl.when(goes_right(p))
            def _():
                block(rail(p), RIGHT, p, h, right).wait_send()

            @pl.when(goes_left(p))
            def _():
                block(rail(p), LEFT, p, h, left).wait_send()

            block(rail(p), ACROSS, p, h, across).wait_send()
            block(rail(p), SIB, p, h, sib).wait_send()
            block(crossed(p), SIB_X, p, h, sib).wait_send()
        rs1(p).wait_send()
        rs2(p).wait_send()

        @pl.when(quad_at(p) != o)
        def _():
            rs3(p).wait_send()

        return carry

    lax.fori_loop(0, line, drain, 0)


def body(tokens, norm_gain, pred_ids, pred_weights, fix_pairs, fix_ids, fix_weights, w_expert):
    peers = lax.axis_size("expert")
    line = peers // QUAD
    tok_rows, feats = tokens.shape
    hidden = w_expert.shape[2]
    width = -(-3 * peers // 128) * 128
    vmem = pl.BlockSpec(memory_space=pltpu.VMEM)
    bf16 = jnp.bfloat16
    return pl.pallas_call(
        functools.partial(kernel, peers),
        out_shape=jax.ShapeDtypeStruct((tok_rows, hidden), jnp.float32),
        in_specs=[vmem] * 7 + [pl.BlockSpec(memory_space=pl.ANY)],
        out_specs=vmem,
        scratch_shapes=[
            pltpu.VMEM((peers, tok_rows, feats // PIECES), bf16),
            pltpu.VMEM((peers, tok_rows, feats // PIECES + width), bf16),
            pltpu.VMEM((feats, hidden), bf16),
            pltpu.VMEM((QUAD * tok_rows, hidden), jnp.float32),
            pltpu.VMEM((RING, QUAD, tok_rows, hidden), jnp.float32),
            pltpu.VMEM((RING, tok_rows, hidden), jnp.float32),
            pltpu.VMEM((tok_rows, hidden), jnp.float32),
            pltpu.VMEM((line, 2, tok_rows, hidden), bf16),
            pltpu.VMEM((line, 2, tok_rows, hidden), bf16),
            pltpu.VMEM((line, tok_rows, hidden), bf16),
            pltpu.VMEM((line, tok_rows, hidden), bf16),
            pltpu.VMEM((line, tok_rows, hidden), bf16),
            pltpu.VMEM((line, tok_rows, hidden), bf16),
            pltpu.SemaphoreType.DMA,
            pltpu.SemaphoreType.DMA((PIECES, 8, line)),
            pltpu.SemaphoreType.DMA((PIECES, peers)),
            pltpu.SemaphoreType.DMA((3, line)),
        ],
        compiler_params=pltpu.CompilerParams(
            collective_id=0, has_side_effects=True, vmem_limit_bytes=62 * 2**20
        ),
    )(
        tokens,
        norm_gain,
        pred_ids.T,
        pred_weights.T,
        fix_pairs.reshape(1, -1),
        fix_ids.reshape(1, -1),
        fix_weights.reshape(1, -1),
        w_expert,
    )


def solution(mesh):
    in_specs = (
        P(("groups", "expert"), None),
        P(),
        P(("groups", "expert"), None),
        P(("groups", "expert"), None),
        P(("groups", "expert")),
        P(("groups", "expert"), None),
        P(("groups", "expert")),
        P("expert", None, None),
    )
    out_specs = P(("groups", "expert"), None)
    return jax.shard_map(body, mesh=mesh, in_specs=in_specs, out_specs=out_specs, check_vma=False)
```

```python
import functools

import jax
import jax.numpy as jnp
from jax import lax
from jax.experimental import pallas as pl
from jax.experimental.pallas import tpu as pltpu
from jax.sharding import PartitionSpec as P

MESH = pl.DeviceIdType.MESH
QUAD = 4
RING = 4
RIGHT, LEFT, ACROSS, SIB, SIB_X, RS1, RS2, RS3 = range(8)
PIECES = 2


def route_columns(peers, width, pid_ref, pw_ref, fp_ref, fid_ref, fw_ref):
    top_k, tok_rows = pid_ref.shape
    fixes = fp_ref.shape[1]
    last = (((1,), (1,)), ((), ()))
    pairs = lax.rem(fp_ref[...], tok_rows * top_k)
    owned = lax.broadcasted_iota(jnp.int32, (tok_rows, fixes), 0) == lax.div(pairs, top_k)
    slots = lax.broadcasted_iota(jnp.int32, (top_k, fixes), 0) == lax.rem(pairs, top_k)
    gone = lax.dot_general(
        jnp.where(slots, 1.0, 0.0),
        jnp.where(owned, 1.0, 0.0),
        last,
        preferred_element_type=jnp.float32,
    )
    keep = jnp.where(gone > 0.5, 0.0, pw_ref[...])
    pids = pid_ref[...]
    row = lax.broadcasted_iota(jnp.int32, (width, tok_rows), 0)
    expert = lax.rem(row, peers)
    piece = lax.div(row, peers)
    fix_row = lax.rem(lax.broadcasted_iota(jnp.int32, (width, fixes), 0), peers)
    hits = jnp.where(fid_ref[...] == fix_row, 1.0, 0.0)
    share = jnp.where(owned, jnp.broadcast_to(fw_ref[...], (tok_rows, fixes)), 0.0)
    total = lax.dot_general(
        hits,
        share,
        last,
        precision=lax.Precision.HIGHEST,
        preferred_element_type=jnp.float32,
    )
    for k in range(top_k):
        total = total + jnp.where(pids[k : k + 1, :] == expert, keep[k : k + 1, :], 0.0)
    high = total.astype(jnp.bfloat16).astype(jnp.float32)
    rest = total - high
    mid = rest.astype(jnp.bfloat16).astype(jnp.float32)
    low = rest - mid
    picked = jnp.where(piece == 0, high, jnp.where(piece == 1, mid, jnp.where(piece == 2, low, 0.0)))
    side = (tok_rows, tok_rows)
    same = lax.broadcasted_iota(jnp.int32, side, 0) == lax.broadcasted_iota(jnp.int32, side, 1)
    turned = lax.dot_general(
        jnp.where(same, 1.0, 0.0).astype(jnp.bfloat16),
        picked.astype(jnp.bfloat16),
        last,
        preferred_element_type=jnp.float32,
    )
    return turned.astype(jnp.bfloat16)


def kernel(
    peers,
    tok_ref,
    gain_ref,
    pid_ref,
    pw_ref,
    fp_ref,
    fid_ref,
    fw_ref,
    w_hbm,
    out_ref,
    xa,
    xb,
    wbuf,
    hbuf,
    ybuf,
    acc,
    own,
    s1,
    r1,
    s2,
    r2,
    s3,
    r3,
    w_sem,
    snd,
    rcv,
    rs_rcv,
):
    line = peers // QUAD
    tok_rows, feats = tok_ref.shape
    hidden = wbuf.shape[1]
    half = feats // PIECES
    width = xb.shape[2] - half
    pieces = (xa, xb)
    group = lax.axis_index("groups")
    me = lax.axis_index("expert")
    o = me // QUAD
    x = (me % QUAD) // 2
    c = me % 2

    def dev(o_, x_, c_):
        return (group, o_ * QUAD + x_ * 2 + c_)

    w_copy = pltpu.make_async_copy(w_hbm.at[0], wbuf, w_sem)
    w_copy.start()

    barrier = pltpu.get_barrier_semaphore()
    pl.semaphore_signal(barrier, inc=1, device_id=dev(o, 1 - x, c), device_id_type=MESH)
    pl.semaphore_signal(barrier, inc=1, device_id=dev(o, x, 1 - c), device_id_type=MESH)
    for d in range(1, line):
        pl.semaphore_signal(
            barrier, inc=1, device_id=dev((o + d) % line, x, c), device_id_type=MESH
        )

    wide = tok_ref[...].astype(jnp.float32)
    scale = lax.rsqrt(jnp.mean(wide * wide, axis=-1, keepdims=True) + 1e-06)
    gain = gain_ref[...].reshape(1, feats)
    xa[me] = (wide[:, :half] * scale * gain[:, :half]).astype(jnp.bfloat16)
    pl.semaphore_wait(barrier, line + 1)

    def quad_at(p):
        m = jnp.minimum(o, line - 1 - o)
        near = jnp.where(p % 2 == 1, o - (p + 1) // 2, o + p // 2)
        far = jnp.where(o < line - 1 - o, p, line - 1 - p)
        return jnp.where(p <= 2 * m, near, far)

    def send(src, dst, kind, recv, device):
        return pltpu.make_async_remote_copy(
            src_ref=src,
            dst_ref=dst,
            send_sem=kind,
            recv_sem=recv,
            device_id=device,
            device_id_type=MESH,
        )

    def block(e, kind, p, h, device):
        piece = pieces[h].at[e]
        return send(piece, piece, snd.at[h, kind, p], rcv.at[h, e], device)

    def rail(p):
        return quad_at(p) * QUAD + x * 2 + c

    def crossed(p):
        return quad_at(p) * QUAD + (1 - x) * 2 + c

    def goes_right(p):
        return (quad_at(p) <= o) & (o < line - 1)

    def goes_left(p):
        return (quad_at(p) >= o) & (o > 0)

    right = dev(jnp.minimum(o + 1, line - 1), x, c)
    left = dev(jnp.maximum(o - 1, 0), x, c)
    across = dev(o, 1 - x, c)
    sib = dev(o, x, 1 - c)

    def rs1(p):
        return send(s1.at[p], r1.at[p], snd.at[0, RS1, p], rs_rcv.at[0, p], sib)

    def rs2(p):
        return send(s2.at[p], r2.at[p], snd.at[0, RS2, p], rs_rcv.at[1, p], across)

    def rs3(p):
        return send(
            s3.at[p], r3.at[o], snd.at[0, RS3, p], rs_rcv.at[2, o], dev(quad_at(p), x, c)
        )

    def forward(p, h):
        e = rail(p)

        @pl.when(goes_right(p))
        def _():
            block(e, RIGHT, p, h, right).start()

        @pl.when(goes_left(p))
        def _():
            block(e, LEFT, p, h, left).start()

        block(e, ACROSS, p, h, across).start()
        block(e, SIB, p, h, sib).start()

    def step_a(p, h):
        block(rail(p), SIB, p, h, sib).wait_recv()
        forward(p, h)

    def step_b(p, h):
        e = crossed(p)
        block(e, SIB_X, p, h, sib).wait_recv()
        block(e, SIB_X, p, h, sib).start()

    rows = QUAD * tok_rows
    tile = 512

    def step_c(p, h):
        q = quad_at(p)
        block(q * QUAD + x * 2 + 1 - c, SIB, p, h, sib).wait_recv()
        block(q * QUAD + (1 - x) * 2 + 1 - c, SIB_X, p, h, sib).wait_recv()
        quad = pl.ds(q * QUAD, QUAD)
        slot = p % RING
        if h == 0:

            @pl.when(p == 0)
            def _():
                w_copy.wait()

        else:
            extra = xb[quad, :, half : half + width].reshape(rows, width)
            lane = lax.broadcasted_iota(jnp.int32, (rows, width), 1)
            mine = (lax.rem(lane, peers) == me) & (lane < 3 * peers)
            share = jnp.sum(jnp.where(mine, extra.astype(jnp.float32), 0.0), axis=1, keepdims=True)

        def column(j, carry):
            cols = pl.ds(pl.multiple_of(j * tile, tile), tile)
            lhs = pieces[h][quad, :, 0:half].reshape(rows, half)
            part = jnp.dot(
                lhs, wbuf[h * half : (h + 1) * half, cols], preferred_element_type=jnp.float32
            )
            if h == 0:
                hbuf[:, cols] = part
            else:
                v = hbuf[:, cols] + part
                y = (v / (1.0 + jnp.exp(-v))).astype(jnp.bfloat16).astype(jnp.float32) * share
                ybuf[slot, :, :, cols] = y.reshape(QUAD, tok_rows, tile)
            return carry

        lax.fori_loop(0, hidden // tile, column, 0)
        if h == 1:
            for k in range(2):
                s1[p, k] = ybuf[slot, k * 2 + 1 - c].astype(jnp.bfloat16)
            rs1(p).start()

    def step_d(p):
        slot = p % RING
        rs1(p).wait_recv()
        s2[p] = (ybuf[slot, (1 - x) * 2 + c] + r1[p, 1 - x].astype(jnp.float32)).astype(jnp.bfloat16)
        rs2(p).start()
        acc[slot] = ybuf[slot, x * 2 + c] + r1[p, x].astype(jnp.float32)

    def step_e(p):
        slot = p % RING
        rs2(p).wait_recv()

        @pl.when(quad_at(p) == o)
        def _():
            own[...] = acc[slot] + r2[p].astype(jnp.float32)

        @pl.when(quad_at(p) != o)
        def _():
            s3[p] = (acc[slot] + r2[p].astype(jnp.float32)).astype(jnp.bfloat16)
            rs3(p).start()

    def step(i, carry):
        for h in range(PIECES):

            @pl.when(i < line)
            def _():
                step_a(i, h)

            @pl.when(i < line + 1)
            def _():
                step_b(i - 1, h)

            if h == 0:

                @pl.when((i >= 2) & (i < line + 2))
                def _():
                    step_c(i - 2, 1)

            else:

                @pl.when(i < line + 1)
                def _():
                    step_c(i - 1, 0)

        @pl.when((i >= 2) & (i < line + 2))
        def _():
            step_d(i - 2)

        @pl.when(i >= 3)
        def _():
            step_e(i - 3)

        return carry

    forward(0, 0)
    xb[me, :, 0:half] = (wide[:, half:] * scale * gain[:, half:]).astype(jnp.bfloat16)
    xb[me, :, half : half + width] = route_columns(
        peers, width, pid_ref, pw_ref, fp_ref, fid_ref, fw_ref
    )
    forward(0, 1)
    lax.fori_loop(1, line + 3, step, 0)

    for d in range(1, line):
        k = (o + d) % line
        send(s3.at[0], r3.at[k], snd.at[0, RS3, 0], rs_rcv.at[2, k], sib).wait_recv()
        own[...] += r3[k].astype(jnp.float32)
    out_ref[...] = own[...]

    def drain(p, carry):
        for h in range(PIECES):

            @pl.when(goes_right(p))
            def _():
                block(rail(p), RIGHT, p, h, right).wait_send()

            @pl.when(goes_left(p))
            def _():
                block(rail(p), LEFT, p, h, left).wait_send()

            block(rail(p), ACROSS, p, h, across).wait_send()
            block(rail(p), SIB, p, h, sib).wait_send()
            block(crossed(p), SIB_X, p, h, sib).wait_send()
        rs1(p).wait_send()
        rs2(p).wait_send()

        @pl.when(quad_at(p) != o)
        def _():
            rs3(p).wait_send()

        return carry

    lax.fori_loop(0, line, drain, 0)


def body(tokens, norm_gain, pred_ids, pred_weights, fix_pairs, fix_ids, fix_weights, w_expert):
    peers = lax.axis_size("expert")
    line = peers // QUAD
    tok_rows, feats = tokens.shape
    hidden = w_expert.shape[2]
    width = -(-3 * peers // 128) * 128
    vmem = pl.BlockSpec(memory_space=pltpu.VMEM)
    bf16 = jnp.bfloat16
    return pl.pallas_call(
        functools.partial(kernel, peers),
        out_shape=jax.ShapeDtypeStruct((tok_rows, hidden), jnp.float32),
        in_specs=[vmem] * 7 + [pl.BlockSpec(memory_space=pl.ANY)],
        out_specs=vmem,
        scratch_shapes=[
            pltpu.VMEM((peers, tok_rows, feats // PIECES), bf16),
            pltpu.VMEM((peers, tok_rows, feats // PIECES + width), bf16),
            pltpu.VMEM((feats, hidden), bf16),
            pltpu.VMEM((QUAD * tok_rows, hidden), jnp.float32),
            pltpu.VMEM((RING, QUAD, tok_rows, hidden), jnp.float32),
            pltpu.VMEM((RING, tok_rows, hidden), jnp.float32),
            pltpu.VMEM((tok_rows, hidden), jnp.float32),
            pltpu.VMEM((line, 2, tok_rows, hidden), bf16),
            pltpu.VMEM((line, 2, tok_rows, hidden), bf16),
            pltpu.VMEM((line, tok_rows, hidden), bf16),
            pltpu.VMEM((line, tok_rows, hidden), bf16),
            pltpu.VMEM((line, tok_rows, hidden), bf16),
            pltpu.VMEM((line, tok_rows, hidden), bf16),
            pltpu.SemaphoreType.DMA,
            pltpu.SemaphoreType.DMA((PIECES, 8, line)),
            pltpu.SemaphoreType.DMA((PIECES, peers)),
            pltpu.SemaphoreType.DMA((3, line)),
        ],
        compiler_params=pltpu.CompilerParams(
            collective_id=0, has_side_effects=True, vmem_limit_bytes=62 * 2**20
        ),
    )(
        tokens,
        norm_gain,
        pred_ids.T,
        pred_weights.T,
        fix_pairs.reshape(1, -1),
        fix_ids.reshape(1, -1),
        fix_weights.reshape(1, -1),
        w_expert,
    )


def solution(mesh):
    in_specs = (
        P(("groups", "expert"), None),
        P(),
        P(("groups", "expert"), None),
        P(("groups", "expert"), None),
        P(("groups", "expert")),
        P(("groups", "expert"), None),
        P(("groups", "expert")),
        P("expert", None, None),
    )
    out_specs = P(("groups", "expert"), None)
    return jax.shard_map(body, mesh=mesh, in_specs=in_specs, out_specs=out_specs, check_vma=False)
```
